32 devices in a mesh: seq: 8 (over z, y), grp: 4 (over x, core).
Axes of the slice: x: 2, y: 2, z: 4, core: 2. Of those that a mesh axis runs over, the one named last changes fastest.
Arguments:
- queries: bfloat16 [4, 4096, 2048], P('grp', 'seq'), may hold values from -12 to 12
- keys: bfloat16 [4, 4096, 2048], P('grp', 'seq'), may hold values from -4 to 4
- values: bfloat16 [4, 4096, 2048], P('grp', 'seq'), may hold values from -6 to 6
- grad_out: bfloat16 [4, 4096, 2048], P('grp', 'seq'), may hold values from -6 to 6
- out_weight: bfloat16 [2048, 2048], replicated, may hold values from -0.125 to 0.125
- segments: int32 [4, 4096], P('grp', 'seq'), may hold values from 0 to 31, never falling along the last dimension, each value on 1 to 512 neighbouring positions
Outputs:
- grad_queries: bfloat16 [4, 4096, 2048], P('grp', 'seq')
- grad_keys: bfloat16 [4, 4096, 2048], P('grp', 'seq')
- grad_values: bfloat16 [4, 4096, 2048], P('grp', 'seq')
- grad_weight: bfloat16 [2048, 2048], P('seq')
The draws below stay inside these ranges and needn't reach their ends.
Inputs may be any that keep to these rules, and one draw needn't show every extreme that they name: `segments`: document numbers never fall along a sequence; every document holds 1 to 512 positions and one holds exactly 512.
All inputs are finite; a program needn't handle non-finite values.
Results may differ from the reference program's by a relative error of at most 0.012.
Values may be sent and summed in bfloat16 or wider, within the bound.
A program may use at most 192 MiB of HBM per device.

```python
import math
import jax
import jax.numpy as jnp
import numpy as np
from jax import lax

HEADS = 16
HEAD_DIM = 128
OUT_COLS = 2048
DOC_MOST = 512
HD = 2048
SEQ = 4096
DOCS = 32
N_GRP = 4


def shared_base(key):
    first, second, third, fourth = jax.random.split(key, 4)
    base = jnp.clip(jax.random.normal(first, (N_GRP, SEQ, HEADS * HEAD_DIM), jnp.float32), -4.0, 4.0)
    direction = jax.random.rademacher(second, (HEADS * HEAD_DIM,), jnp.float32)
    marked = jax.random.uniform(third, (N_GRP, SEQ, 1), jnp.float32) < 0.03125
    strength = jax.random.uniform(fourth, (N_GRP, SEQ, 1), jnp.float32, 1.5, 2.5)
    keyed = jnp.where(marked, 0.3 * base + strength * direction, base)
    return (keyed, direction)


def draw_keys(key, part):
    keyed, direction = shared_base(key)
    return keyed.astype(jnp.bfloat16)


def draw_queries(key, part):
    keyed, direction = shared_base(key)
    key = jax.random.fold_in(key, 5)
    first = jax.random.fold_in(key, 0)
    fourth = jax.random.fold_in(key, 3)
    fresh = jnp.clip(jax.random.normal(first, (N_GRP, SEQ, HEADS * HEAD_DIM), jnp.float32), -4.0, 4.0)
    pull = jax.random.uniform(fourth, (N_GRP, SEQ, 1), jnp.float32, 0.0, 0.15)
    return (fresh + pull * direction).astype(jnp.bfloat16)


def block_levels(own_key, dims, shards, least, top_value):
    gain = 1.0
    for dim, blocks in shards:
        heights = jax.random.uniform(jax.random.fold_in(jax.random.fold_in(own_key, 6), dim), (blocks,), jnp.float32, least / len(shards), top_value / len(shards))
        gain = gain * jnp.repeat(jnp.exp(heights), dims[dim] // blocks).reshape((-1,) + (1,) * (len(dims) - 1 - dim))
    return gain


def split_up(amount, total, reach, lean):
    loads = [(1 << 20) // math.isqrt(grade ** lean) + 1 for grade in range(2, amount + 1)]
    surplus, holding = total - reach - (amount - 1), [1] * (amount - 1)
    while surplus > 0:
        candidates = [i for i in range(amount - 1) if holding[i] < reach]
        pool, budget = sum([loads[i] for i in candidates]), surplus
        for i in candidates:
            extra = min(reach - holding[i], max(1, budget * loads[i] // pool), surplus)
            holding[i] = holding[i] + extra
            surplus = surplus - extra
    return np.array([reach] + holding)


def uneven(own_key, number_of, total, bound, lean):
    if number_of == 2:
        one = jax.random.randint(own_key, (), max(1, total - bound), min(bound, total - 1) + 1)
        return jnp.stack([one, total - one])
    lengths = jnp.asarray(split_up(number_of, total, bound, lean), jnp.int32)
    couples = (number_of - 1) // 2
    giver, taker = lengths[1:1 + 2 * couples:2], lengths[2:2 + 2 * couples:2]
    room = jnp.minimum(giver - 1, bound - taker)
    moved = jax.random.randint(jax.random.fold_in(own_key, 1), (couples,), 0, 1 << 20) % (room + 1)
    lengths = lengths.at[1:1 + 2 * couples:2].set(giver - moved).at[2:2 + 2 * couples:2].set(taker + moved)
    return lengths[jax.random.permutation(jax.random.fold_in(own_key, 2), number_of)]


def centred(rng, shape, deviation, bound, pieces=(), kind=jnp.bfloat16):
    entries = jax.random.normal(rng, shape, jnp.float32) * deviation
    if len(pieces) > 0:
        entries = block_levels(rng, shape, pieces, -0.22, 0.18) * entries
    return jnp.clip(entries, min=-bound, max=bound).astype(kind)


def setup_inputs(seed: int = 0) -> dict:
    splits = jax.random.split(jax.random.key(seed), 7)
    queries = draw_queries(jax.random.fold_in(splits[6], 71), 0)
    keys = draw_keys(jax.random.fold_in(splits[6], 71), 0)
    values = centred(splits[2], (N_GRP, SEQ, HD), 1.0, 6.0, ((0, 4), (1, 8)))
    grad_out = centred(splits[3], (N_GRP, SEQ, OUT_COLS), 1.0, 6.0, ((0, 4), (1, 8)))
    out_weight = centred(splits[4], (HD, OUT_COLS), HD ** -0.5, 0.125)
    segments = jax.vmap(lambda own: jnp.searchsorted(jnp.cumsum(uneven(own, DOCS, SEQ, DOC_MOST, 2)), jnp.arange(SEQ), side="right"))(jax.random.split(splits[5], N_GRP)).reshape((N_GRP, SEQ)).astype(jnp.int32)
    return dict(queries=queries, keys=keys, values=values, grad_out=grad_out, out_weight=out_weight, segments=segments)


def alibi_slopes():
    head_ids = jnp.arange(HEADS, dtype=jnp.float32)
    return 2.0 ** (-(17.0 + head_ids) / 4.0)


def to_bfloat(source):
    return lax.optimization_barrier(source.astype(jnp.bfloat16)).astype(jnp.float32)


def reference(queries, keys, values, grad_out, out_weight, segments):
    score_scale = HEAD_DIM ** -0.5
    block_rows = min(256, SEQ)
    window_rows = min(block_rows + DOC_MOST, SEQ)
    block_count = SEQ // block_rows
    slopes = alibi_slopes()

    def one_group(group_args):
        group_q, group_k, group_v, group_g, group_s = group_args
        grad_context = lax.dot_general(group_g, out_weight, (((1,), (1,)), ((), ())),
                                       preferred_element_type=jnp.float32).astype(jnp.bfloat16)

        def tiles(block_id):
            q_start = (block_id * block_rows).astype(jnp.int32)
            k_start = jnp.maximum(q_start + block_rows - window_rows, 0).astype(jnp.int32)
            query_block = lax.dynamic_slice_in_dim(group_q, q_start, block_rows, 0).astype(jnp.float32).reshape(block_rows, HEADS, HEAD_DIM)
            key_block = lax.dynamic_slice_in_dim(group_k, k_start, window_rows, 0).astype(jnp.float32).reshape(window_rows, HEADS, HEAD_DIM)
            value_block = lax.dynamic_slice_in_dim(group_v, k_start, window_rows, 0).astype(jnp.float32).reshape(window_rows, HEADS, HEAD_DIM)
            seg_q = lax.dynamic_slice_in_dim(group_s, q_start, block_rows, 0)
            seg_k = lax.dynamic_slice_in_dim(group_s, k_start, window_rows, 0)
            q_pos = q_start + jnp.arange(block_rows, dtype=jnp.int32)
            k_pos = k_start + jnp.arange(window_rows, dtype=jnp.int32)
            allowed = ((seg_q[:, None] == seg_k[None, :]) & (k_pos[None, :] <= q_pos[:, None]))[None]
            distance = (q_pos[:, None] - k_pos[None, :]).astype(jnp.float32)
            scores = jnp.einsum("qhd,khd->hqk", query_block, key_block) * score_scale - slopes[:, None, None] * distance[None]
            return q_start, k_start, query_block, key_block, value_block, allowed, scores

        def forward_step(block_id, carry):
            context_all, lse_all = carry
            q_start, k_start, query_block, key_block, value_block, allowed, scores = tiles(block_id.astype(jnp.int32))
            masked = jnp.where(allowed, scores, -1e30)
            top = jnp.max(masked, axis=-1)
            total = jnp.sum(jnp.where(allowed, jnp.exp(scores - top[:, :, None]), 0.0), axis=-1)
            lse = top + jnp.log(total)
            probs = jnp.where(allowed, jnp.exp(scores - lse[:, :, None]), 0.0)
            weights = to_bfloat(probs)
            context = jnp.einsum("hqk,khd->qhd", weights, value_block).astype(jnp.bfloat16).reshape(block_rows, HD)
            context_all = lax.dynamic_update_slice_in_dim(context_all, context, q_start, 0)
            lse_all = lax.dynamic_update_slice_in_dim(lse_all, lse, q_start, 1)
            return context_all, lse_all

        context_all, lse_all = lax.fori_loop(
            0, block_count, forward_step,
            (jnp.zeros((SEQ, HD), jnp.bfloat16), jnp.zeros((HEADS, SEQ), jnp.float32)))

        def backward_step(block_id, carry):
            grad_q_all, grad_k_all, grad_v_all = carry
            q_start, k_start, query_block, key_block, value_block, allowed, scores = tiles(block_id.astype(jnp.int32))
            lse = lax.dynamic_slice_in_dim(lse_all, q_start, block_rows, 1)
            probs = jnp.where(allowed, jnp.exp(scores - lse[:, :, None]), 0.0)
            weights = to_bfloat(probs)
            grad_block = lax.dynamic_slice_in_dim(grad_context, q_start, block_rows, 0).astype(jnp.float32).reshape(block_rows, HEADS, HEAD_DIM)
            context_block = lax.dynamic_slice_in_dim(context_all, q_start, block_rows, 0).astype(jnp.float32).reshape(block_rows, HEADS, HEAD_DIM)
            delta = jnp.sum(grad_block * context_block, axis=-1).T
            dprob = jnp.einsum("qhd,khd->hqk", grad_block, value_block)
            dscore = to_bfloat(probs * (dprob - delta[:, :, None]))
            grad_q = (jnp.einsum("hqk,khd->qhd", dscore, key_block) * score_scale).astype(jnp.bfloat16).reshape(block_rows, HD)
            grad_k = (jnp.einsum("hqk,qhd->khd", dscore, query_block) * score_scale).reshape(window_rows, HD)
            grad_v = jnp.einsum("hqk,qhd->khd", weights, grad_block).reshape(window_rows, HD)
            grad_q_all = lax.dynamic_update_slice_in_dim(grad_q_all, grad_q, q_start, 0)
            old_k = lax.dynamic_slice_in_dim(grad_k_all, k_start, window_rows, 0)
            old_v = lax.dynamic_slice_in_dim(grad_v_all, k_start, window_rows, 0)
            grad_k_all = lax.dynamic_update_slice_in_dim(grad_k_all, old_k + grad_k, k_start, 0)
            grad_v_all = lax.dynamic_update_slice_in_dim(grad_v_all, old_v + grad_v, k_start, 0)
            return grad_q_all, grad_k_all, grad_v_all

        grad_q_all, grad_k_all, grad_v_all = lax.fori_loop(
            0, block_count, backward_step,
            (jnp.zeros((SEQ, HD), jnp.bfloat16), jnp.zeros((SEQ, HD), jnp.float32), jnp.zeros((SEQ, HD), jnp.float32)))
        weight_term = jnp.dot(context_all.astype(jnp.float32).T, group_g.astype(jnp.float32))
        return grad_q_all, grad_k_all.astype(jnp.bfloat16), grad_v_all.astype(jnp.bfloat16), weight_term

    grad_queries, grad_keys, grad_values, weight_terms = lax.map(one_group, (queries, keys, values, grad_out, segments))
    grad_weight = jnp.sum(weight_terms, axis=0).astype(jnp.bfloat16)
    return (grad_queries, grad_keys, grad_values, grad_weight)
```

```python
import jax
import jax.numpy as jnp
from jax import lax
from jax.sharding import PartitionSpec as P

HEADS = 16


def from_behind(shard, axis, by):
    length = lax.axis_size(axis)
    pairs = [(i, i + by) for i in range(length) if 0 <= i + by < length]
    return lax.ppermute(shard, axis, pairs)


def alibi_slopes():
    head_ids = jnp.arange(HEADS, dtype=jnp.float32)
    return 2.0 ** (-(17.0 + head_ids) / 4.0)


def local(queries, keys, values, grad_out, out_weight, segments):
    query_rows = queries[0]
    key_rows = keys[0]
    value_rows = values[0]
    grad_rows = grad_out[0]
    seg_local = segments[0]
    tok_rows, full_width = query_rows.shape
    head_dim = full_width // HEADS
    score_scale = head_dim ** (-0.5)
    shard_index = lax.axis_index("seq")
    positions = jnp.arange(tok_rows, dtype=jnp.int32)
    query_pos = shard_index * tok_rows + positions
    slopes = alibi_slopes()
    query_heads = query_rows.reshape(tok_rows, HEADS, head_dim)
    fetched = [(key_rows, value_rows, seg_local)]
    hop_index = 1
    fetched.append(from_behind((key_rows, value_rows, seg_local), "seq", hop_index))

    def tile_mask(hop_index):
        seg_part = fetched[hop_index][2]
        key_pos = (shard_index - hop_index) * tok_rows + positions
        allowed = (
            (seg_local[:, None] == seg_part[None, :])
            & (key_pos[None, :] <= query_pos[:, None])
            & (shard_index >= hop_index)
        )
        return (allowed[None], key_pos)

    def tile_scores(hop_index):
        key_part, value_part, seg_part = fetched[hop_index]
        allowed, key_pos = tile_mask(hop_index)
        distance = (query_pos[:, None] - key_pos[None, :]).astype(jnp.float32)
        key_heads = key_part.reshape(tok_rows, HEADS, head_dim)
        value_heads = value_part.reshape(tok_rows, HEADS, head_dim)
        scores = (
            jnp.einsum("qhd,khd->hqk", query_heads, key_heads, preferred_element_type=jnp.float32)
            * score_scale
        )
        scores = scores - slopes[:, None, None] * distance[None]
        return (scores, allowed, key_heads, value_heads)

    def stat_maker(hop_index):
        scores, allowed, key_heads, value_heads = tile_scores(hop_index)
        top = jnp.max(jnp.where(allowed, scores, -1e30), axis=-1)
        total = jnp.sum(jnp.where(allowed, jnp.exp(scores - top[:, :, None]), 0.0), axis=-1)
        return (scores, top, total)

    first_scores, running_top, running_total = stat_maker(0)
    kept_scores = [first_scores]
    hop_index = 1
    hop_scores, new_top_part, new_total = stat_maker(hop_index)
    kept_scores.append(hop_scores)
    merged_top = jnp.maximum(running_top, new_top_part)
    running_total = running_total * jnp.exp(running_top - merged_top) + new_total * jnp.exp(
        new_top_part - merged_top
    )
    log_total = merged_top + jnp.log(running_total)

    def context_maker(hop_index):
        allowed, key_pos = tile_mask(hop_index)
        value_heads = fetched[hop_index][1].reshape(tok_rows, HEADS, head_dim)
        weights = jnp.where(
            allowed, jnp.exp(kept_scores[hop_index] - log_total[:, :, None]), 0.0
        ).astype(jnp.bfloat16)
        return jnp.einsum("hqk,khd->qhd", weights, value_heads, preferred_element_type=jnp.float32)

    context_sum = context_maker(0)
    hop_index = 1
    context_sum = context_sum + context_maker(hop_index)
    context = context_sum.astype(jnp.bfloat16).reshape(tok_rows, full_width)
    weight_term = lax.dot_general(
        context, grad_rows, (((0,), (0,)), ((), ())), preferred_element_type=jnp.float32
    ).astype(jnp.bfloat16)
    weight_term = lax.psum_scatter(weight_term, "grp", scatter_dimension=1, tiled=True)
    weight_term = lax.psum_scatter(weight_term, "seq", scatter_dimension=0, tiled=True)
    grad_weight = lax.all_gather(weight_term, "grp", axis=1, tiled=True)
    grad_context = lax.dot_general(
        grad_rows, out_weight, (((1,), (1,)), ((), ())), preferred_element_type=jnp.float32
    ).astype(jnp.bfloat16)
    grad_heads = grad_context.reshape(tok_rows, HEADS, head_dim)
    context_heads = context.reshape(tok_rows, HEADS, head_dim)
    delta = jnp.sum(grad_heads.astype(jnp.float32) * context_heads.astype(jnp.float32), axis=-1).T

    def backward_maker(hop_index):
        scores, allowed, key_heads, value_heads = tile_scores(hop_index)
        probs = jnp.where(allowed, jnp.exp(scores - log_total[:, :, None]), 0.0)
        weights = probs.astype(jnp.bfloat16)
        dprob = jnp.einsum(
            "qhd,khd->hqk", grad_heads, value_heads, preferred_element_type=jnp.float32
        )
        dscore = (probs * (dprob - delta[:, :, None])).astype(jnp.bfloat16)
        grad_q = jnp.einsum("hqk,khd->qhd", dscore, key_heads, preferred_element_type=jnp.float32)
        grad_k = (
            jnp.einsum("hqk,qhd->khd", dscore, query_heads, preferred_element_type=jnp.float32)
            * score_scale
        )
        grad_v = jnp.einsum("hqk,qhd->khd", weights, grad_heads, preferred_element_type=jnp.float32)
        return (grad_q, grad_k.reshape(tok_rows, full_width), grad_v.reshape(tok_rows, full_width))

    grad_q_sum, first_k, first_v = backward_maker(0)
    parts_k = [first_k]
    parts_v = [first_v]
    hop_index = 1
    grad_q_part, grad_k_part, grad_v_part = backward_maker(hop_index)
    grad_q_sum = grad_q_sum + grad_q_part
    parts_k.append(grad_k_part)
    parts_v.append(grad_v_part)
    total_k = parts_k[0]
    total_v = parts_v[0]
    hop_index = 1
    back_k, back_v = from_behind(
        (parts_k[hop_index].astype(jnp.bfloat16), parts_v[hop_index].astype(jnp.bfloat16)),
        "seq",
        -hop_index,
    )
    total_k = total_k + back_k.astype(jnp.float32)
    total_v = total_v + back_v.astype(jnp.float32)
    grad_query = (grad_q_sum * score_scale).astype(jnp.bfloat16).reshape(tok_rows, full_width)
    grad_key = total_k.astype(jnp.bfloat16)
    grad_value = total_v.astype(jnp.bfloat16)
    return (grad_query[None], grad_key[None], grad_value[None], grad_weight)


def solution(mesh):
    placed = (
        P("grp", "seq", None),
        P("grp", "seq", None),
        P("grp", "seq", None),
        P("grp", "seq", None),
        P(),
        P("grp", "seq"),
    )
    return jax.shard_map(
        local,
        mesh=mesh,
        in_specs=placed,
        out_specs=(
            P("grp", "seq", None),
            P("grp", "seq", None),
            P("grp", "seq", None),
            P("seq", None),
        ),
        check_vma=False,
    )
```

```python
import functools

import jax
import jax.numpy as jnp
from jax import lax
from jax.experimental import pallas as pl
from jax.experimental.pallas import tpu as pltpu
from jax.sharding import PartitionSpec as P

HEADS = 16
CHUNKS = 4
WEIGHT_PARTS = 2
LOW = -1e30
PARAMS = dict(vmem_limit_bytes=40 * 1024 * 1024)


def from_behind(shard, axis, by):
    length = lax.axis_size(axis)
    pairs = [(i, i + by) for i in range(length) if 0 <= i + by < length]
    return lax.ppermute(shard, axis, pairs)


def alibi_slopes():
    head_ids = jnp.arange(HEADS, dtype=jnp.float32)
    return 2.0 ** (-(17.0 + head_ids) / 4.0)


def dot_nt(a, b):
    return lax.dot_general(a, b, (((1,), (1,)), ((), ())), preferred_element_type=jnp.float32)


def dot_nn(a, b):
    return lax.dot_general(a, b, (((1,), (0,)), ((), ())), preferred_element_type=jnp.float32)


def dot_tn(a, b):
    return lax.dot_general(a, b, (((0,), (0,)), ((), ())), preferred_element_type=jnp.float32)


def tile_scores(query, key, slope, scale, first_col):
    columns = key.shape[0]
    places = lax.broadcasted_iota(jnp.int32, (1, columns), 1) + first_col
    return dot_nt(query, key) * scale + slope * places.astype(jnp.float32)


def own_mask(seg_col, seg_row):
    rows, columns = seg_col.shape[0], seg_row.shape[1]
    row = lax.broadcasted_iota(jnp.int32, (rows, columns), 0)
    column = lax.broadcasted_iota(jnp.int32, (rows, columns), 1)
    return (seg_col == seg_row) & (column <= row)


def own_forward(scale, slopes, seg_col, seg_row, q, k, v, out, stat):
    rows = q.shape[0]
    slope = slopes[pl.program_id(0)]
    scores = tile_scores(q[...], k[...], slope, scale, rows)
    scores = jnp.where(own_mask(seg_col[...], seg_row[...]), scores, LOW)
    top = jnp.max(scores, axis=1, keepdims=True)
    probs = jnp.exp(scores - top)
    total = jnp.sum(probs, axis=1, keepdims=True)
    mixed = dot_nn(probs.astype(jnp.bfloat16), v[...])
    out[...] = mixed / total
    stat[...] = jnp.broadcast_to(top + jnp.log(total), stat.shape)


def hop_step(scale, base, slopes, seg_col, seg_row, q, kv, grad, out, stat, context, lse, delta, grad_q, grad_kv):
    slope = slopes[pl.program_id(0) + base]
    query, key, value, grad_rows = q[...], kv[0], kv[1], grad[...]
    scores = tile_scores(query, key, slope, scale, 0)
    scores = jnp.where(seg_col[...] == seg_row[...], scores, LOW)
    own = stat[:, 0:1]
    top = jnp.maximum(jnp.max(scores, axis=1, keepdims=True), own)
    raw = jnp.exp(scores - top)
    own_part = jnp.exp(own - top)
    total = own_part + jnp.sum(raw, axis=1, keepdims=True)
    share = 1.0 / total
    probs = raw * share
    weights = probs.astype(jnp.bfloat16)
    mixed = out[...] * (own_part * share) + dot_nn(weights, value)
    rounded = mixed.astype(jnp.bfloat16)
    context[...] = rounded
    row_delta = jnp.sum(
        rounded.astype(jnp.float32) * grad_rows.astype(jnp.float32), axis=1, keepdims=True
    )
    lse[...] = jnp.broadcast_to(top + jnp.log(total), lse.shape)
    delta[...] = jnp.broadcast_to(row_delta, delta.shape)
    dscore = (probs * (dot_nt(grad_rows, value) - row_delta)).astype(jnp.bfloat16)
    grad_q[...] = dot_nn(dscore, key)
    grad_kv[0] = (dot_tn(dscore, query) * scale).astype(jnp.bfloat16)
    grad_kv[1] = dot_tn(weights, grad_rows).astype(jnp.bfloat16)


def own_backward(scale, base, slopes, seg_col, seg_row, q, k, v, grad, lse, delta, hop_q, grad_q, grad_kv):
    rows = q.shape[0]
    slope = slopes[pl.program_id(0) + base]
    query, key, value, grad_rows = q[...], k[...], v[...], grad[...]
    scores = tile_scores(query, key, slope, scale, rows)
    scores = jnp.where(own_mask(seg_col[...], seg_row[...]), scores, LOW)
    probs = jnp.exp(scores - lse[:, 0:1])
    weights = probs.astype(jnp.bfloat16)
    dscore = (probs * (dot_nt(grad_rows, value) - delta[:, 0:1])).astype(jnp.bfloat16)
    grad_q[...] = ((dot_nn(dscore, key) + hop_q[...]) * scale).astype(jnp.bfloat16)
    grad_kv[0] = dot_tn(dscore, query) * scale
    grad_kv[1] = dot_tn(weights, grad_rows)


def local(queries, keys, values, grad_out, out_weight, segments):
    query_rows = queries[0]
    key_rows = keys[0]
    value_rows = values[0]
    grad_rows = grad_out[0]
    tok_rows, full_width = query_rows.shape
    head_dim = full_width // HEADS
    scale = head_dim ** (-0.5)
    chunk_heads = HEADS // CHUNKS
    width = chunk_heads * head_dim
    slopes = alibi_slopes()
    seg_col = segments.reshape(tok_rows, 1)
    seg_row = segments
    seg_behind = from_behind(segments, "seq", 1)
    seg_behind = jnp.where(lax.axis_index("seq") > 0, seg_behind, -1)

    arrived = []
    for part in range(CHUNKS):
        columns = slice(part * width, (part + 1) * width)
        both = jnp.stack([key_rows[:, columns], value_rows[:, columns]])
        arrived.append(from_behind(both, "seq", 1))

    slope_spec = pl.BlockSpec(memory_space=pltpu.SMEM)
    col_spec = pl.BlockSpec((tok_rows, 1), lambda h: (0, 0))
    row_spec = pl.BlockSpec((1, tok_rows), lambda h: (0, 0))
    part_spec = pl.BlockSpec((tok_rows, head_dim), lambda h: (0, h))
    pair_spec = pl.BlockSpec((2, tok_rows, head_dim), lambda h: (0, 0, h))

    def head_spec(base):
        return pl.BlockSpec((tok_rows, head_dim), lambda h: (0, base + h))

    def cost(heads, dots):
        pairs = heads * tok_rows * tok_rows
        return pl.CostEstimate(
            flops=2 * dots * pairs * head_dim,
            bytes_accessed=16 * heads * tok_rows * head_dim,
            transcendentals=pairs,
        )

    full = jax.ShapeDtypeStruct((tok_rows, full_width), jnp.float32)
    part_f32 = jax.ShapeDtypeStruct((tok_rows, width), jnp.float32)
    part_bf16 = jax.ShapeDtypeStruct((tok_rows, width), jnp.bfloat16)

    grad_context = lax.dot_general(
        grad_rows, out_weight, (((1,), (1,)), ((), ())), preferred_element_type=jnp.float32
    ).astype(jnp.bfloat16)

    own_out, own_stat = pl.pallas_call(
        functools.partial(own_forward, scale),
        grid=(HEADS,),
        in_specs=[slope_spec, col_spec, row_spec] + [head_spec(0)] * 3,
        out_specs=[head_spec(0)] * 2,
        out_shape=[full, full],
        compiler_params=pltpu.CompilerParams(**PARAMS),
        cost_estimate=cost(HEADS, 2),
        name="own_forward",
    )(slopes, seg_col, seg_row, query_rows, key_rows, value_rows)

    hops, backs, terms, pieces = [], [], [], []
    for part in range(CHUNKS):
        base = part * chunk_heads
        own_spec = head_spec(base)
        hop = pl.pallas_call(
            functools.partial(hop_step, scale, base),
            grid=(chunk_heads,),
            in_specs=[slope_spec, col_spec, row_spec, own_spec, pair_spec, own_spec, own_spec, own_spec],
            out_specs=[part_spec] * 4 + [pair_spec],
            out_shape=[
                part_bf16,
                part_f32,
                part_f32,
                part_f32,
                jax.ShapeDtypeStruct((2, tok_rows, width), jnp.bfloat16),
            ],
            compiler_params=pltpu.CompilerParams(**PARAMS),
            cost_estimate=cost(chunk_heads, 6),
            name="hop_step",
        )(slopes, seg_col, seg_behind, query_rows, arrived[part], grad_context, own_out, own_stat)
        hops.append(hop)
        backs.append(from_behind(hop[4], "seq", -1))
        pieces.append(hop[0])
        if (part + 1) % (CHUNKS // WEIGHT_PARTS) == 0:
            context = jnp.concatenate(pieces, axis=1)
            pieces = []
            term = lax.dot_general(
                context, grad_rows, (((0,), (0,)), ((), ())), preferred_element_type=jnp.float32
            ).astype(jnp.bfloat16)
            terms.append(lax.psum_scatter(term, "grp", scatter_dimension=1, tiled=True))

    weight_term = lax.psum_scatter(
        jnp.concatenate(terms, axis=0), "seq", scatter_dimension=0, tiled=True
    )
    grad_weight = lax.all_gather(weight_term, "grp", axis=1, tiled=True)

    grads_q, grads_k, grads_v = [], [], []
    for part in range(CHUNKS):
        base = part * chunk_heads
        own_spec = head_spec(base)
        _, lse, delta, hop_q, _ = hops[part]
        grad_q, grad_kv = pl.pallas_call(
            functools.partial(own_backward, scale, base),
            grid=(chunk_heads,),
            in_specs=[slope_spec, col_spec, row_spec] + [own_spec] * 4 + [part_spec] * 3,
            out_specs=[part_spec, pair_spec],
            out_shape=[part_bf16, jax.ShapeDtypeStruct((2, tok_rows, width), jnp.float32)],
            compiler_params=pltpu.CompilerParams(**PARAMS),
            cost_estimate=cost(chunk_heads, 5),
            name="own_backward",
        )(slopes, seg_col, seg_row, query_rows, key_rows, value_rows, grad_context, lse, delta, hop_q)
        total = (grad_kv + backs[part].astype(jnp.float32)).astype(jnp.bfloat16)
        grads_q.append(grad_q)
        grads_k.append(total[0])
        grads_v.append(total[1])
    grad_query = jnp.concatenate(grads_q, axis=1)
    grad_key = jnp.concatenate(grads_k, axis=1)
    grad_value = jnp.concatenate(grads_v, axis=1)
    return (grad_query[None], grad_key[None], grad_value[None], grad_weight)


def solution(mesh):
    placed = (
        P("grp", "seq", None),
        P("grp", "seq", None),
        P("grp", "seq", None),
        P("grp", "seq", None),
        P(),
        P("grp", "seq"),
    )
    return jax.shard_map(
        local,
        mesh=mesh,
        in_specs=placed,
        out_specs=(
            P("grp", "seq", None),
            P("grp", "seq", None),
            P("grp", "seq", None),
            P("seq", None),
        ),
        check_vma=False,
    )
```

```python
import functools

import jax
import jax.numpy as jnp
from jax import lax
from jax.experimental import pallas as pl
from jax.experimental.pallas import tpu as pltpu
from jax.sharding import PartitionSpec as P

HEADS = 16
CHUNKS = 2
WEIGHT_PARTS = 2
LOW = -1e30
PARAMS = dict(vmem_limit_bytes=40 * 1024 * 1024)


def from_behind(shard, axis, by):
    length = lax.axis_size(axis)
    pairs = [(i, i + by) for i in range(length) if 0 <= i + by < length]
    return lax.ppermute(shard, axis, pairs)


def alibi_slopes():
    head_ids = jnp.arange(HEADS, dtype=jnp.float32)
    return 2.0 ** (-(17.0 + head_ids) / 4.0)


def halve(parts, axis, bit):
    length = lax.axis_size(axis)
    mine = (lax.axis_index(axis) // bit) % 2
    sent = lax.dynamic_index_in_dim(parts, 1 - mine, 0, keepdims=False)
    kept = lax.dynamic_index_in_dim(parts, mine, 0, keepdims=False)
    came = lax.ppermute(sent, axis, [(i, i ^ bit) for i in range(length)])
    return (kept.astype(jnp.float32) + came.astype(jnp.float32)).astype(jnp.bfloat16)


def scatter_columns(term, axis):
    bit, blocks = 1, lax.axis_size(axis)
    rows, columns = term.shape
    parts = term.reshape(rows, blocks, columns // blocks).transpose(1, 0, 2)
    while bit < lax.axis_size(axis):
        blocks = blocks // 2
        shape = (blocks, 2) + parts.shape[1:]
        parts = halve(jnp.swapaxes(parts.reshape(shape), 0, 1), axis, bit)
        bit = bit * 2
    return parts[0]


def scatter_rows(term, axis):
    bit, blocks = 1, lax.axis_size(axis)
    parts = term.reshape(blocks, term.shape[0] // blocks, term.shape[1])
    while bit < lax.axis_size(axis):
        blocks = blocks // 2
        shape = (blocks, 2) + parts.shape[1:]
        parts = halve(jnp.swapaxes(parts.reshape(shape), 0, 1), axis, bit)
        bit = bit * 2
    return parts[0]


def dot_nt(a, b):
    return lax.dot_general(a, b, (((1,), (1,)), ((), ())), preferred_element_type=jnp.float32)


def dot_nn(a, b):
    return lax.dot_general(a, b, (((1,), (0,)), ((), ())), preferred_element_type=jnp.float32)


def dot_tn(a, b):
    return lax.dot_general(a, b, (((0,), (0,)), ((), ())), preferred_element_type=jnp.float32)


def tile_scores(query, key, slope, scale, first_col):
    columns = key.shape[0]
    places = lax.broadcasted_iota(jnp.int32, (1, columns), 1) + first_col
    return dot_nt(query, key) * scale + slope * places.astype(jnp.float32)


def own_mask(seg_col, seg_row):
    rows, columns = seg_col.shape[0], seg_row.shape[1]
    row = lax.broadcasted_iota(jnp.int32, (rows, columns), 0)
    column = lax.broadcasted_iota(jnp.int32, (rows, columns), 1)
    return (seg_col == seg_row) & (column <= row)


def own_forward(scale, slopes, seg_col, seg_row, q, k, v, out, stat):
    rows = q.shape[0]
    slope = slopes[pl.program_id(0)]
    scores = tile_scores(q[...], k[...], slope, scale, rows)
    scores = jnp.where(own_mask(seg_col[...], seg_row[...]), scores, LOW)
    top = jnp.max(scores, axis=1, keepdims=True)
    probs = jnp.exp(scores - top)
    total = jnp.sum(probs, axis=1, keepdims=True)
    mixed = dot_nn(probs.astype(jnp.bfloat16), v[...])
    out[...] = mixed / total
    stat[...] = jnp.broadcast_to(top + jnp.log(total), stat.shape)


def hop_step(scale, base, slopes, seg_col, seg_row, q, kv, grad, out, stat, context, lse, delta, grad_q, grad_kv):
    slope = slopes[pl.program_id(0) + base]
    query, key, value, grad_rows = q[...], kv[0], kv[1], grad[...]
    scores = tile_scores(query, key, slope, scale, 0)
    scores = jnp.where(seg_col[...] == seg_row[...], scores, LOW)
    own = stat[:, 0:1]
    top = jnp.maximum(jnp.max(scores, axis=1, keepdims=True), own)
    raw = jnp.exp(scores - top)
    own_part = jnp.exp(own - top)
    total = own_part + jnp.sum(raw, axis=1, keepdims=True)
    share = 1.0 / total
    probs = raw * share
    weights = probs.astype(jnp.bfloat16)
    mixed = out[...] * (own_part * share) + dot_nn(weights, value)
    rounded = mixed.astype(jnp.bfloat16)
    context[...] = rounded
    row_delta = jnp.sum(
        rounded.astype(jnp.float32) * grad_rows.astype(jnp.float32), axis=1, keepdims=True
    )
    lse[...] = jnp.broadcast_to(top + jnp.log(total), lse.shape)
    delta[...] = jnp.broadcast_to(row_delta, delta.shape)
    dscore = (probs * (dot_nt(grad_rows, value) - row_delta)).astype(jnp.bfloat16)
    grad_q[...] = dot_nn(dscore, key)
    grad_kv[0] = (dot_tn(dscore, query) * scale).astype(jnp.bfloat16)
    grad_kv[1] = dot_tn(weights, grad_rows).astype(jnp.bfloat16)


def own_backward(scale, base, slopes, seg_col, seg_row, q, k, v, grad, lse, delta, hop_q, grad_q, grad_kv):
    rows = q.shape[0]
    slope = slopes[pl.program_id(0) + base]
    query, key, value, grad_rows = q[...], k[...], v[...], grad[...]
    scores = tile_scores(query, key, slope, scale, rows)
    scores = jnp.where(own_mask(seg_col[...], seg_row[...]), scores, LOW)
    probs = jnp.exp(scores - lse[:, 0:1])
    weights = probs.astype(jnp.bfloat16)
    dscore = (probs * (dot_nt(grad_rows, value) - delta[:, 0:1])).astype(jnp.bfloat16)
    grad_q[...] = ((dot_nn(dscore, key) + hop_q[...]) * scale).astype(jnp.bfloat16)
    grad_kv[0] = dot_tn(dscore, query) * scale
    grad_kv[1] = dot_tn(weights, grad_rows)


def local(queries, keys, values, grad_out, out_weight, segments):
    query_rows = queries[0]
    key_rows = keys[0]
    value_rows = values[0]
    grad_rows = grad_out[0]
    tok_rows, full_width = query_rows.shape
    head_dim = full_width // HEADS
    scale = head_dim ** (-0.5)
    chunk_heads = HEADS // CHUNKS
    width = chunk_heads * head_dim
    slopes = alibi_slopes()
    seg_col = segments.reshape(tok_rows, 1)
    seg_row = segments
    seg_behind = from_behind(segments, "seq", 1)
    seg_behind = jnp.where(lax.axis_index("seq") > 0, seg_behind, -1)

    arrived = []
    for part in range(CHUNKS):
        columns = slice(part * width, (part + 1) * width)
        both = jnp.stack([key_rows[:, columns], value_rows[:, columns]])
        arrived.append(from_behind(both, "seq", 1))

    slope_spec = pl.BlockSpec(memory_space=pltpu.SMEM)
    col_spec = pl.BlockSpec((tok_rows, 1), lambda h: (0, 0))
    row_spec = pl.BlockSpec((1, tok_rows), lambda h: (0, 0))
    part_spec = pl.BlockSpec((tok_rows, head_dim), lambda h: (0, h))
    pair_spec = pl.BlockSpec((2, tok_rows, head_dim), lambda h: (0, 0, h))

    def head_spec(base):
        return pl.BlockSpec((tok_rows, head_dim), lambda h: (0, base + h))

    def cost(heads, dots):
        pairs = heads * tok_rows * tok_rows
        return pl.CostEstimate(
            flops=dots * pairs,
            bytes_accessed=heads * tok_rows * head_dim,
            transcendentals=0,
        )

    full = jax.ShapeDtypeStruct((tok_rows, full_width), jnp.float32)
    part_f32 = jax.ShapeDtypeStruct((tok_rows, width), jnp.float32)
    part_bf16 = jax.ShapeDtypeStruct((tok_rows, width), jnp.bfloat16)

    grad_context = lax.dot_general(
        grad_rows, out_weight, (((1,), (1,)), ((), ())), preferred_element_type=jnp.float32
    ).astype(jnp.bfloat16)

    own_out, own_stat = pl.pallas_call(
        functools.partial(own_forward, scale),
        grid=(HEADS,),
        in_specs=[slope_spec, col_spec, row_spec] + [head_spec(0)] * 3,
        out_specs=[head_spec(0)] * 2,
        out_shape=[full, full],
        compiler_params=pltpu.CompilerParams(**PARAMS),
        cost_estimate=cost(HEADS, 2),
        name="own_forward",
    )(slopes, seg_col, seg_row, query_rows, key_rows, value_rows)

    hops, backs, terms, pieces = [], [], [], []
    for part in range(CHUNKS):
        base = part * chunk_heads
        own_spec = head_spec(base)
        hop = pl.pallas_call(
            functools.partial(hop_step, scale, base),
            grid=(chunk_heads,),
            in_specs=[slope_spec, col_spec, row_spec, own_spec, pair_spec, own_spec, own_spec, own_spec],
            out_specs=[part_spec] * 4 + [pair_spec],
            out_shape=[
                part_bf16,
                part_f32,
                part_f32,
                part_f32,
                jax.ShapeDtypeStruct((2, tok_rows, width), jnp.bfloat16),
            ],
            compiler_params=pltpu.CompilerParams(**PARAMS),
            cost_estimate=cost(chunk_heads, 6),
            name="hop_step",
        )(slopes, seg_col, seg_behind, query_rows, arrived[part], grad_context, own_out, own_stat)
        hops.append(hop)
        backs.append(from_behind(hop[4], "seq", -1))
        pieces.append(hop[0])
        if (part + 1) % (CHUNKS // WEIGHT_PARTS) == 0:
            context = jnp.concatenate(pieces, axis=1)
            pieces = []
            term = lax.dot_general(
                context, grad_rows, (((0,), (0,)), ((), ())), preferred_element_type=jnp.float32
            ).astype(jnp.bfloat16)
            terms.append(scatter_columns(term, "grp"))

    weight_term = scatter_rows(jnp.concatenate(terms, axis=0), "seq")
    grad_weight = lax.all_gather(weight_term, "grp", axis=1, tiled=True)

    grads_q, grads_k, grads_v = [], [], []
    for part in range(CHUNKS):
        base = part * chunk_heads
        own_spec = head_spec(base)
        _, lse, delta, hop_q, _ = hops[part]
        grad_q, grad_kv = pl.pallas_call(
            functools.partial(own_backward, scale, base),
            grid=(chunk_heads,),
            in_specs=[slope_spec, col_spec, row_spec] + [own_spec] * 4 + [part_spec] * 3,
            out_specs=[part_spec, pair_spec],
            out_shape=[part_bf16, jax.ShapeDtypeStruct((2, tok_rows, width), jnp.float32)],
            compiler_params=pltpu.CompilerParams(**PARAMS),
            cost_estimate=cost(chunk_heads, 5),
            name="own_backward",
        )(slopes, seg_col, seg_row, query_rows, key_rows, value_rows, grad_context, lse, delta, hop_q)
        total = (grad_kv + backs[part].astype(jnp.float32)).astype(jnp.bfloat16)
        grads_q.append(grad_q)
        grads_k.append(total[0])
        grads_v.append(total[1])
    grad_query = jnp.concatenate(grads_q, axis=1)
    grad_key = jnp.concatenate(grads_k, axis=1)
    grad_value = jnp.concatenate(grads_v, axis=1)
    return (grad_query[None], grad_key[None], grad_value[None], grad_weight)


def solution(mesh):
    placed = (
        P("grp", "seq", None),
        P("grp", "seq", None),
        P("grp", "seq", None),
        P("grp", "seq", None),
        P(),
        P("grp", "seq"),
    )
    return jax.shard_map(
        local,
        mesh=mesh,
        in_specs=placed,
        out_specs=(
            P("grp", "seq", None),
            P("grp", "seq", None),
            P("grp", "seq", None),
            P("seq", None),
        ),
        check_vma=False,
    )
```

```python
import functools

import jax
import jax.numpy as jnp
from jax import lax
from jax.experimental import pallas as pl
from jax.experimental.pallas import tpu as pltpu
from jax.sharding import PartitionSpec as P

HEADS = 16
CHUNKS = 2
LOW = -1e30
PARAMS = dict(vmem_limit_bytes=40 * 1024 * 1024)


def from_behind(shard, axis, by):
    length = lax.axis_size(axis)
    pairs = [(i, i + by) for i in range(length) if 0 <= i + by < length]
    return lax.ppermute(shard, axis, pairs)


def alibi_slopes():
    head_ids = jnp.arange(HEADS, dtype=jnp.float32)
    return 2.0 ** (-(17.0 + head_ids) / 4.0)


def halve(parts, axis, bit):
    length = lax.axis_size(axis)
    mine = (lax.axis_index(axis) // bit) % 2
    sent = lax.dynamic_index_in_dim(parts, 1 - mine, 0, keepdims=False)
    kept = lax.dynamic_index_in_dim(parts, mine, 0, keepdims=False)
    came = lax.ppermute(sent, axis, [(i, i ^ bit) for i in range(length)])
    return (kept.astype(jnp.float32) + came.astype(jnp.float32)).astype(jnp.bfloat16)


def split_columns(term, axis):
    blocks = lax.axis_size(axis)
    rows, columns = term.shape
    parts = term.reshape(rows, blocks // 2, 2, columns // blocks).transpose(2, 1, 0, 3)
    return halve(parts, axis, 1)


def finish_columns(parts, axis):
    bit, blocks = 2, parts.shape[0]
    while bit < lax.axis_size(axis):
        blocks = blocks // 2
        shape = (blocks, 2) + parts.shape[1:]
        parts = halve(jnp.swapaxes(parts.reshape(shape), 0, 1), axis, bit)
        bit = bit * 2
    return parts[0]


def scatter_rows(term, axis, late):
    length = lax.axis_size(axis)
    bits = [1 << n for n in range(length.bit_length() - 1)]
    shape = (2,) * len(bits) + (term.shape[0] // length, term.shape[1])
    parts = term.reshape(shape)
    left = bits[::-1]
    for step, bit in enumerate(bits[1:] + bits[:1]):
        if step == 1:
            parts, late = lax.optimization_barrier((parts, late))
        parts = halve(jnp.moveaxis(parts, left.index(bit), 0), axis, bit)
        left.remove(bit)
    return parts, late


def dot_nt(a, b):
    return lax.dot_general(a, b, (((1,), (1,)), ((), ())), preferred_element_type=jnp.float32)


def dot_nn(a, b):
    return lax.dot_general(a, b, (((1,), (0,)), ((), ())), preferred_element_type=jnp.float32)


def dot_tn(a, b):
    return lax.dot_general(a, b, (((0,), (0,)), ((), ())), preferred_element_type=jnp.float32)


def tile_scores(query, key, slope, scale, first_col):
    columns = key.shape[0]
    places = lax.broadcasted_iota(jnp.int32, (1, columns), 1) + first_col
    return dot_nt(query, key) * scale + slope * places.astype(jnp.float32)


def own_mask(seg_col, seg_row):
    rows, columns = seg_col.shape[0], seg_row.shape[1]
    row = lax.broadcasted_iota(jnp.int32, (rows, columns), 0)
    column = lax.broadcasted_iota(jnp.int32, (rows, columns), 1)
    return (seg_col == seg_row) & (column <= row)


def own_forward(scale, slopes, seg_col, seg_row, q, k, v, out, stat):
    rows = q.shape[0]
    slope = slopes[pl.program_id(0)]
    scores = tile_scores(q[...], k[...], slope, scale, rows)
    scores = jnp.where(own_mask(seg_col[...], seg_row[...]), scores, LOW)
    top = jnp.max(scores, axis=1, keepdims=True)
    probs = jnp.exp(scores - top)
    total = jnp.sum(probs, axis=1, keepdims=True)
    mixed = dot_nn(probs.astype(jnp.bfloat16), v[...])
    out[...] = mixed / total
    stat[...] = jnp.broadcast_to(top + jnp.log(total), stat.shape)


def hop_step(scale, base, slopes, seg_col, seg_row, q, kv, grad, out, stat, context, lse, delta, grad_q, grad_kv):
    slope = slopes[pl.program_id(0) + base]
    query, key, value, grad_rows = q[...], kv[0], kv[1], grad[...]
    scores = tile_scores(query, key, slope, scale, 0)
    scores = jnp.where(seg_col[...] == seg_row[...], scores, LOW)
    own = stat[:, 0:1]
    top = jnp.maximum(jnp.max(scores, axis=1, keepdims=True), own)
    raw = jnp.exp(scores - top)
    own_part = jnp.exp(own - top)
    total = own_part + jnp.sum(raw, axis=1, keepdims=True)
    share = 1.0 / total
    probs = raw * share
    weights = probs.astype(jnp.bfloat16)
    mixed = out[...] * (own_part * share) + dot_nn(weights, value)
    rounded = mixed.astype(jnp.bfloat16)
    context[...] = rounded
    row_delta = jnp.sum(
        rounded.astype(jnp.float32) * grad_rows.astype(jnp.float32), axis=1, keepdims=True
    )
    lse[...] = jnp.broadcast_to(top + jnp.log(total), lse.shape)
    delta[...] = jnp.broadcast_to(row_delta, delta.shape)
    dscore = (probs * (dot_nt(grad_rows, value) - row_delta)).astype(jnp.bfloat16)
    grad_q[...] = dot_nn(dscore, key)
    grad_kv[0] = (dot_tn(dscore, query) * scale).astype(jnp.bfloat16)
    grad_kv[1] = dot_tn(weights, grad_rows).astype(jnp.bfloat16)


def own_backward(scale, base, slopes, seg_col, seg_row, q, k, v, grad, lse, delta, hop_q, grad_q, grad_kv):
    rows = q.shape[0]
    slope = slopes[pl.program_id(0) + base]
    query, key, value, grad_rows = q[...], k[...], v[...], grad[...]
    scores = tile_scores(query, key, slope, scale, rows)
    scores = jnp.where(own_mask(seg_col[...], seg_row[...]), scores, LOW)
    probs = jnp.exp(scores - lse[:, 0:1])
    weights = probs.astype(jnp.bfloat16)
    dscore = (probs * (dot_nt(grad_rows, value) - delta[:, 0:1])).astype(jnp.bfloat16)
    grad_q[...] = ((dot_nn(dscore, key) + hop_q[...]) * scale).astype(jnp.bfloat16)
    grad_kv[0] = dot_tn(dscore, query) * scale
    grad_kv[1] = dot_tn(weights, grad_rows)


def local(queries, keys, values, grad_out, out_weight, segments):
    query_rows = queries[0]
    key_rows = keys[0]
    value_rows = values[0]
    grad_rows = grad_out[0]
    tok_rows, full_width = query_rows.shape
    head_dim = full_width // HEADS
    scale = head_dim ** (-0.5)
    chunk_heads = HEADS // CHUNKS
    width = chunk_heads * head_dim
    slopes = alibi_slopes()
    seg_col = segments.reshape(tok_rows, 1)
    seg_row = segments
    seg_behind = from_behind(segments, "seq", 1)
    seg_behind = jnp.where(lax.axis_index("seq") > 0, seg_behind, -1)

    arrived = []
    for part in range(CHUNKS):
        columns = slice(part * width, (part + 1) * width)
        both = jnp.stack([key_rows[:, columns], value_rows[:, columns]])
        arrived.append(from_behind(both, "seq", 1))

    slope_spec = pl.BlockSpec(memory_space=pltpu.SMEM)
    col_spec = pl.BlockSpec((tok_rows, 1), lambda h: (0, 0))
    row_spec = pl.BlockSpec((1, tok_rows), lambda h: (0, 0))
    part_spec = pl.BlockSpec((tok_rows, head_dim), lambda h: (0, h))
    pair_spec = pl.BlockSpec((2, tok_rows, head_dim), lambda h: (0, 0, h))

    def head_spec(base):
        return pl.BlockSpec((tok_rows, head_dim), lambda h: (0, base + h))

    def cost(heads, dots):
        pairs = heads * tok_rows * tok_rows
        return pl.CostEstimate(
            flops=dots * pairs,
            bytes_accessed=heads * tok_rows * head_dim,
            transcendentals=0,
        )

    full = jax.ShapeDtypeStruct((tok_rows, full_width), jnp.float32)
    part_f32 = jax.ShapeDtypeStruct((tok_rows, width), jnp.float32)
    part_bf16 = jax.ShapeDtypeStruct((tok_rows, width), jnp.bfloat16)

    grad_context = lax.dot_general(
        grad_rows, out_weight, (((1,), (1,)), ((), ())), preferred_element_type=jnp.float32
    ).astype(jnp.bfloat16)

    own_out, own_stat = pl.pallas_call(
        functools.partial(own_forward, scale),
        grid=(HEADS,),
        in_specs=[slope_spec, col_spec, row_spec] + [head_spec(0)] * 3,
        out_specs=[head_spec(0)] * 2,
        out_shape=[full, full],
        compiler_params=pltpu.CompilerParams(**PARAMS),
        cost_estimate=cost(HEADS, 2),
        name="own_forward",
    )(slopes, seg_col, seg_row, query_rows, key_rows, value_rows)

    hops, backs, terms = [], [], []
    held = None
    for part in range(CHUNKS):
        base = part * chunk_heads
        own_spec = head_spec(base)
        came = arrived[part]
        if held is not None:
            terms.append(finish_columns(held, "grp"))
        hop = pl.pallas_call(
            functools.partial(hop_step, scale, base),
            grid=(chunk_heads,),
            in_specs=[slope_spec, col_spec, row_spec, own_spec, pair_spec, own_spec, own_spec, own_spec],
            out_specs=[part_spec] * 4 + [pair_spec],
            out_shape=[
                part_bf16,
                part_f32,
                part_f32,
                part_f32,
                jax.ShapeDtypeStruct((2, tok_rows, width), jnp.bfloat16),
            ],
            compiler_params=pltpu.CompilerParams(**PARAMS),
            cost_estimate=cost(chunk_heads, 6),
            name="hop_step",
        )(slopes, seg_col, seg_behind, query_rows, came, grad_context, own_out, own_stat)
        hops.append(hop)
        backs.append(from_behind(hop[4], "seq", -1))
        context = hop[0]
        if part > 0:
            context, backs[part - 1] = lax.optimization_barrier((context, backs[part - 1]))
        term = lax.dot_general(
            context, grad_rows, (((0,), (0,)), ((), ())), preferred_element_type=jnp.float32
        ).astype(jnp.bfloat16)
        held = split_columns(term, "grp")
    terms.append(finish_columns(held, "grp"))

    grads_q, grads_k, grads_v, own_terms = [], [], [], []
    for part in range(CHUNKS):
        base = part * chunk_heads
        own_spec = head_spec(base)
        _, lse, delta, hop_q, _ = hops[part]
        grad_q, grad_kv = pl.pallas_call(
            functools.partial(own_backward, scale, base),
            grid=(chunk_heads,),
            in_specs=[slope_spec, col_spec, row_spec] + [own_spec] * 4 + [part_spec] * 3,
            out_specs=[part_spec, pair_spec],
            out_shape=[part_bf16, jax.ShapeDtypeStruct((2, tok_rows, width), jnp.float32)],
            compiler_params=pltpu.CompilerParams(**PARAMS),
            cost_estimate=cost(chunk_heads, 5),
            name="own_backward",
        )(slopes, seg_col, seg_row, query_rows, key_rows, value_rows, grad_context, lse, delta, hop_q)
        own_terms.append(grad_kv)
        grads_q.append(grad_q)
    terms, own_terms = lax.optimization_barrier((terms, own_terms))
    weight_term, backs[-1] = scatter_rows(jnp.concatenate(terms, axis=0), "seq", backs[-1])
    grad_weight = lax.all_gather(weight_term, "grp", axis=1, tiled=True)
    for part in range(CHUNKS):
        total = (own_terms[part] + backs[part].astype(jnp.float32)).astype(jnp.bfloat16)
        grads_k.append(total[0])
        grads_v.append(total[1])
    grad_query = jnp.concatenate(grads_q, axis=1)
    grad_key = jnp.concatenate(grads_k, axis=1)
    grad_value = jnp.concatenate(grads_v, axis=1)
    return (grad_query[None], grad_key[None], grad_value[None], grad_weight)


def solution(mesh):
    placed = (
        P("grp", "seq", None),
        P("grp", "seq", None),
        P("grp", "seq", None),
        P("grp", "seq", None),
        P(),
        P("grp", "seq"),
    )
    return jax.shard_map(
        local,
        mesh=mesh,
        in_specs=placed,
        out_specs=(
            P("grp", "seq", None),
            P("grp", "seq", None),
            P("grp", "seq", None),
            P("seq", None),
        ),
        check_vma=False,
    )
```

```python
import functools

import jax
import jax.numpy as jnp
from jax import lax
from jax.experimental import pallas as pl
from jax.experimental.pallas import tpu as pltpu
from jax.sharding import PartitionSpec as P

HEADS = 16
CHUNKS = 2
LOW = -1e30
PARAMS = dict(vmem_limit_bytes=40 * 1024 * 1024)


def from_behind(shard, axis, by):
    length = lax.axis_size(axis)
    pairs = [(i, i + by) for i in range(length) if 0 <= i + by < length]
    return lax.ppermute(shard, axis, pairs)


def alibi_slopes():
    head_ids = jnp.arange(HEADS, dtype=jnp.float32)
    return 2.0 ** (-(17.0 + head_ids) / 4.0)


def halve(parts, axis, bit):
    length = lax.axis_size(axis)
    mine = (lax.axis_index(axis) // bit) % 2
    sent = lax.dynamic_index_in_dim(parts, 1 - mine, 0, keepdims=False)
    kept = lax.dynamic_index_in_dim(parts, mine, 0, keepdims=False)
    came = lax.ppermute(sent, axis, [(i, i ^ bit) for i in range(length)])
    return (kept.astype(jnp.float32) + came.astype(jnp.float32)).astype(jnp.bfloat16)


def split_columns(term, axis):
    blocks = lax.axis_size(axis)
    rows, columns = term.shape
    parts = term.reshape(rows, blocks, columns // blocks).transpose(1, 0, 2)
    shape = (blocks // 2, 2) + parts.shape[1:]
    return halve(jnp.swapaxes(parts.reshape(shape), 0, 1), axis, 1)


def finish_columns(parts, axis):
    bit, blocks = 2, parts.shape[0]
    while bit < lax.axis_size(axis):
        blocks = blocks // 2
        shape = (blocks, 2) + parts.shape[1:]
        parts = halve(jnp.swapaxes(parts.reshape(shape), 0, 1), axis, bit)
        bit = bit * 2
    return parts[0]


def scatter_rows(term, axis, late):
    length = lax.axis_size(axis)
    bits = [1 << n for n in range(length.bit_length() - 1)]
    shape = (2,) * len(bits) + (term.shape[0] // length, term.shape[1])
    parts = term.reshape(shape)
    left = bits[::-1]
    for step, bit in enumerate(bits[1:] + bits[:1]):
        if step == 1:
            parts, late = lax.optimization_barrier((parts, late))
        parts = halve(jnp.moveaxis(parts, left.index(bit), 0), axis, bit)
        left.remove(bit)
    return parts, late


def dot_nt(a, b):
    return lax.dot_general(a, b, (((1,), (1,)), ((), ())), preferred_element_type=jnp.float32)


def dot_nn(a, b):
    return lax.dot_general(a, b, (((1,), (0,)), ((), ())), preferred_element_type=jnp.float32)


def dot_tn(a, b):
    return lax.dot_general(a, b, (((0,), (0,)), ((), ())), preferred_element_type=jnp.float32)


def tile_scores(query, key, slope, scale, first_col):
    columns = key.shape[0]
    places = lax.broadcasted_iota(jnp.int32, (1, columns), 1) + first_col
    return dot_nt(query, key) * scale + slope * places.astype(jnp.float32)


def own_mask(seg_col, seg_row):
    rows, columns = seg_col.shape[0], seg_row.shape[1]
    row = lax.broadcasted_iota(jnp.int32, (rows, columns), 0)
    column = lax.broadcasted_iota(jnp.int32, (rows, columns), 1)
    return (seg_col == seg_row) & (column <= row)


def own_forward(scale, slopes, seg_col, seg_row, q, k, v, out, stat):
    rows = q.shape[0]
    slope = slopes[pl.program_id(0)]
    scores = tile_scores(q[...], k[...], slope, scale, rows)
    scores = jnp.where(own_mask(seg_col[...], seg_row[...]), scores, LOW)
    top = jnp.max(scores, axis=1, keepdims=True)
    probs = jnp.exp(scores - top)
    total = jnp.sum(probs, axis=1, keepdims=True)
    mixed = dot_nn(probs.astype(jnp.bfloat16), v[...])
    out[...] = mixed / total
    stat[...] = jnp.broadcast_to(top + jnp.log(total), stat.shape)


def hop_step(scale, base, slopes, seg_col, seg_row, q, kv, grad, out, stat, context, lse, delta, grad_q, grad_kv):
    slope = slopes[pl.program_id(0) + base]
    query, key, value, grad_rows = q[...], kv[0], kv[1], grad[...]
    scores = tile_scores(query, key, slope, scale, 0)
    scores = jnp.where(seg_col[...] == seg_row[...], scores, LOW)
    own = stat[:, 0:1]
    top = jnp.maximum(jnp.max(scores, axis=1, keepdims=True), own)
    raw = jnp.exp(scores - top)
    own_part = jnp.exp(own - top)
    total = own_part + jnp.sum(raw, axis=1, keepdims=True)
    share = 1.0 / total
    probs = raw * share
    weights = probs.astype(jnp.bfloat16)
    mixed = out[...] * (own_part * share) + dot_nn(weights, value)
    rounded = mixed.astype(jnp.bfloat16)
    context[...] = rounded
    row_delta = jnp.sum(
        rounded.astype(jnp.float32) * grad_rows.astype(jnp.float32), axis=1, keepdims=True
    )
    lse[...] = jnp.broadcast_to(top + jnp.log(total), lse.shape)
    delta[...] = jnp.broadcast_to(row_delta, delta.shape)
    dscore = (probs * (dot_nt(grad_rows, value) - row_delta)).astype(jnp.bfloat16)
    grad_q[...] = dot_nn(dscore, key)
    grad_kv[0] = (dot_tn(dscore, query) * scale).astype(jnp.bfloat16)
    grad_kv[1] = dot_tn(weights, grad_rows).astype(jnp.bfloat16)


def own_backward(scale, base, slopes, seg_col, seg_row, q, k, v, grad, lse, delta, hop_q, grad_q, grad_kv):
    rows = q.shape[0]
    slope = slopes[pl.program_id(0) + base]
    query, key, value, grad_rows = q[...], k[...], v[...], grad[...]
    scores = tile_scores(query, key, slope, scale, rows)
    scores = jnp.where(own_mask(seg_col[...], seg_row[...]), scores, LOW)
    probs = jnp.exp(scores - lse[:, 0:1])
    weights = probs.astype(jnp.bfloat16)
    dscore = (probs * (dot_nt(grad_rows, value) - delta[:, 0:1])).astype(jnp.bfloat16)
    grad_q[...] = ((dot_nn(dscore, key) + hop_q[...]) * scale).astype(jnp.bfloat16)
    grad_kv[0] = dot_tn(dscore, query) * scale
    grad_kv[1] = dot_tn(weights, grad_rows)


def local(queries, keys, values, grad_out, out_weight, segments):
    query_rows = queries[0]
    key_rows = keys[0]
    value_rows = values[0]
    grad_rows = grad_out[0]
    tok_rows, full_width = query_rows.shape
    head_dim = full_width // HEADS
    scale = head_dim ** (-0.5)
    chunk_heads = HEADS // CHUNKS
    width = chunk_heads * head_dim
    slopes = alibi_slopes()
    seg_col = segments.reshape(tok_rows, 1)
    seg_row = segments
    seg_behind = from_behind(segments, "seq", 1)
    seg_behind = jnp.where(lax.axis_index("seq") > 0, seg_behind, -1)

    arrived = []
    for part in range(CHUNKS):
        columns = slice(part * width, (part + 1) * width)
        both = jnp.stack([key_rows[:, columns], value_rows[:, columns]])
        arrived.append(from_behind(both, "seq", 1))

    slope_spec = pl.BlockSpec(memory_space=pltpu.SMEM)
    col_spec = pl.BlockSpec((tok_rows, 1), lambda h: (0, 0))
    row_spec = pl.BlockSpec((1, tok_rows), lambda h: (0, 0))
    part_spec = pl.BlockSpec((tok_rows, head_dim), lambda h: (0, h))
    pair_spec = pl.BlockSpec((2, tok_rows, head_dim), lambda h: (0, 0, h))

    def head_spec(base):
        return pl.BlockSpec((tok_rows, head_dim), lambda h: (0, base + h))

    def cost(heads, dots):
        pairs = heads * tok_rows * tok_rows
        return pl.CostEstimate(
            flops=dots * pairs,
            bytes_accessed=heads * tok_rows * head_dim,
            transcendentals=0,
        )

    full = jax.ShapeDtypeStruct((tok_rows, full_width), jnp.float32)
    part_f32 = jax.ShapeDtypeStruct((tok_rows, width), jnp.float32)
    part_bf16 = jax.ShapeDtypeStruct((tok_rows, width), jnp.bfloat16)

    grad_context = lax.dot_general(
        grad_rows, out_weight, (((1,), (1,)), ((), ())), preferred_element_type=jnp.float32
    ).astype(jnp.bfloat16)

    own_out, own_stat = pl.pallas_call(
        functools.partial(own_forward, scale),
        grid=(HEADS,),
        in_specs=[slope_spec, col_spec, row_spec] + [head_spec(0)] * 3,
        out_specs=[head_spec(0)] * 2,
        out_shape=[full, full],
        compiler_params=pltpu.CompilerParams(**PARAMS),
        cost_estimate=cost(HEADS, 2),
        name="own_forward",
    )(slopes, seg_col, seg_row, query_rows, key_rows, value_rows)

    hops, backs, terms = [], [], []
    held = None
    for part in range(CHUNKS):
        base = part * chunk_heads
        own_spec = head_spec(base)
        came = arrived[part]
        if held is not None:
            terms.append(finish_columns(held, "grp"))
        hop = pl.pallas_call(
            functools.partial(hop_step, scale, base),
            grid=(chunk_heads,),
            in_specs=[slope_spec, col_spec, row_spec, own_spec, pair_spec, own_spec, own_spec, own_spec],
            out_specs=[part_spec] * 4 + [pair_spec],
            out_shape=[
                part_bf16,
                part_f32,
                part_f32,
                part_f32,
                jax.ShapeDtypeStruct((2, tok_rows, width), jnp.bfloat16),
            ],
            compiler_params=pltpu.CompilerParams(**PARAMS),
            cost_estimate=cost(chunk_heads, 6),
            name="hop_step",
        )(slopes, seg_col, seg_behind, query_rows, came, grad_context, own_out, own_stat)
        hops.append(hop)
        backs.append(from_behind(hop[4], "seq", -1))
        context = hop[0]
        if part > 0:
            context, backs[part - 1] = lax.optimization_barrier((context, backs[part - 1]))
        term = lax.dot_general(
            context, grad_rows, (((0,), (0,)), ((), ())), preferred_element_type=jnp.float32
        ).astype(jnp.bfloat16)
        held = split_columns(term, "grp")
    terms.append(finish_columns(held, "grp"))

    grads_q, grads_k, grads_v, own_terms = [], [], [], []
    for part in range(CHUNKS):
        base = part * chunk_heads
        own_spec = head_spec(base)
        _, lse, delta, hop_q, _ = hops[part]
        grad_q, grad_kv = pl.pallas_call(
            functools.partial(own_backward, scale, base),
            grid=(chunk_heads,),
            in_specs=[slope_spec, col_spec, row_spec] + [own_spec] * 4 + [part_spec] * 3,
            out_specs=[part_spec, pair_spec],
            out_shape=[part_bf16, jax.ShapeDtypeStruct((2, tok_rows, width), jnp.float32)],
            compiler_params=pltpu.CompilerParams(**PARAMS),
            cost_estimate=cost(chunk_heads, 5),
            name="own_backward",
        )(slopes, seg_col, seg_row, query_rows, key_rows, value_rows, grad_context, lse, delta, hop_q)
        own_terms.append(grad_kv)
        grads_q.append(grad_q)
    terms, own_terms = lax.optimization_barrier((terms, own_terms))
    weight_term, backs[-1] = scatter_rows(jnp.concatenate(terms, axis=0), "seq", backs[-1])
    grad_weight = lax.all_gather(weight_term, "grp", axis=1, tiled=True)
    for part in range(CHUNKS):
        total = (own_terms[part] + backs[part].astype(jnp.float32)).astype(jnp.bfloat16)
        grads_k.append(total[0])
        grads_v.append(total[1])
    grad_query = jnp.concatenate(grads_q, axis=1)
    grad_key = jnp.concatenate(grads_k, axis=1)
    grad_value = jnp.concatenate(grads_v, axis=1)
    return (grad_query[None], grad_key[None], grad_value[None], grad_weight)


def solution(mesh):
    placed = (
        P("grp", "seq", None),
        P("grp", "seq", None),
        P("grp", "seq", None),
        P("grp", "seq", None),
        P(),
        P("grp", "seq"),
    )
    return jax.shard_map(
        local,
        mesh=mesh,
        in_specs=placed,
        out_specs=(
            P("grp", "seq", None),
            P("grp", "seq", None),
            P("grp", "seq", None),
            P("seq", None),
        ),
        check_vma=False,
    )
```
